256 devices in a mesh: seq: 64 (over z, y, core), tp: 4 (over x).
Axes of the slice: x: 4, y: 4, z: 8, core: 2. Of those that a mesh axis runs over, the one named last changes fastest.
Arguments:
- residual: bfloat16 [16384, 4096], P('seq', 'tp'), may hold values from -6 to 6
- cotangent: bfloat16 [16384, 4096], P('seq', 'tp'), may hold values from -6 to 6
- kept_slots: int32 [4096], P('seq'), may hold values from -1 to 255, as said below
- query: bfloat16 [4096, 2048], P('seq', 'tp'), may hold values from -6 to 6
- rotated_key_slots: bfloat16 [4096, 512], P('seq', 'tp'), may hold values from -6 to 6
- kept_value_slots: bfloat16 [4096, 512], P('seq', 'tp'), may hold values from -6 to 6
- router: float32 [4096], P('seq'), may hold values from 0.2 to 1
- out_weight: bfloat16 [2048, 4096], P('tp'), may hold values from -0.125 to 0.125
Outputs:
- updated: bfloat16 [16384, 4096], P('seq', 'tp')
- grad_query: bfloat16 [4096, 2048], P('seq', 'tp')
- key_gradient_slots: bfloat16 [4096, 512], P('seq', 'tp')
- value_gradient_slots: bfloat16 [4096, 512], P('seq', 'tp')
- grad_router: float32 [4096], P('seq')
- grad_weight: bfloat16 [2048, 4096], P('tp', 'seq')
The draws below stay inside these ranges and needn't reach their ends.
Inputs may be any that keep to these rules, and one draw needn't show every extreme that they name: `kept_slots`: slot c of shard s holds the in-shard position of the shard's c-th kept token, positions rising with c; after the shard's last kept token its slots hold -1. 2048 slots are live in all, and some shard has all 64 slots live.
All inputs are finite; a program needn't handle non-finite values.
Results may differ from the reference program's by a relative error of at most 0.03.
Values may be sent and summed in bfloat16 or wider, within the bound.
No kernel may reach another device: no remote copies, remote signals or barrier semaphores. Data moves between devices by JAX's collectives and lax.ppermute only.
A program may use at most 64 MiB of HBM per device.

```python
import math
import jax
import jax.numpy as jnp
from jax import lax

D = 4096
HEAD_SIZE = 128
QUERY_HEADS = 16
KEY_VALUE_HEADS = 4
TOK_DEV = 256
RK = 32
MOST = 64
TOKENS = 16384
KEPT_TOKENS = 2048
TOTAL_SLOTS = 4096
N_SEQ = 64


def draw_kept_slots(key, part):
    key = jax.random.fold_in(key, 11)
    key_pairs, key_order, key_ranks = jax.random.split(key, 3)
    pair_count = N_SEQ // 2
    pair_shift = jax.random.randint(key_pairs, (pair_count,), 0, RK + 1)
    pair_shift = pair_shift.at[0].set(RK)
    shard_order = jax.random.permutation(key_order, N_SEQ)
    pair_counts = jnp.stack([RK + pair_shift, RK - pair_shift], axis=1).reshape(N_SEQ)
    counts = jnp.zeros((N_SEQ,), jnp.int32).at[shard_order].set(pair_counts.astype(jnp.int32))
    positions = jnp.arange(TOK_DEV, dtype=jnp.int32)
    rank_keys = jax.random.randint(key_ranks, (N_SEQ, TOK_DEV), 0, (1 << 30) // TOK_DEV) * TOK_DEV + positions[None, :]
    position_rank = jnp.argsort(jnp.argsort(rank_keys, axis=1), axis=1)
    chosen = position_rank < counts[:, None]
    sort_keys = jnp.where(chosen, positions[None, :], TOK_DEV + positions[None, :])
    picked = jnp.sort(sort_keys, axis=1)[:, :MOST]
    slot_table = jnp.where(picked < TOK_DEV, picked, -1)
    return slot_table.reshape(TOTAL_SLOTS).astype(jnp.int32)


def draw_query(key, part):
    key = jax.random.fold_in(key, 7)
    initial_sample = jnp.clip(jax.random.normal(key, (TOTAL_SLOTS, QUERY_HEADS * HEAD_SIZE), jnp.float32), -6.0, 6.0)
    return initial_sample.astype(jnp.bfloat16)


def draw_rotated_key_slots(key, part):
    key = jax.random.fold_in(key, 8)
    initial_sample = jnp.clip(jax.random.normal(key, (TOTAL_SLOTS, KEY_VALUE_HEADS * HEAD_SIZE), jnp.float32), -6.0, 6.0)
    return initial_sample.astype(jnp.bfloat16)


def shard_levels(own_key, extent, shards, low, top_value):
    level = 1.0
    for dim, shards_of in shards:
        steps = jax.random.uniform(jax.random.fold_in(jax.random.fold_in(own_key, 6), dim), (shards_of,), jnp.float32, low / len(shards), top_value / len(shards))
        level = level * jnp.repeat(jnp.exp(steps), extent[dim] // shards_of).reshape((-1,) + (1,) * (len(extent) - 1 - dim))
    return level


def scatter_about(own_key, extent, spread, limit, pieces=(), held_as=jnp.bfloat16):
    entries = jax.random.normal(own_key, extent, jnp.float32) * spread
    if len(pieces) > 0:
        entries = shard_levels(own_key, extent, pieces, -0.22, 0.18) * entries
    return jnp.clip(entries, min=-limit, max=limit).astype(held_as)


def setup_inputs(seed: int = 0) -> dict:
    arg_keys = jax.random.split(jax.random.key(seed), 9)
    residual = scatter_about(arg_keys[0], (TOKENS, D), 1.0, 6.0, ((0, 64), (1, 4)))
    cotangent = scatter_about(arg_keys[1], (TOKENS, D), 1.0, 6.0, ((0, 64), (1, 4)))
    kept_slots = draw_kept_slots(jax.random.fold_in(arg_keys[8], 71), 0)
    query = draw_query(jax.random.fold_in(arg_keys[8], 71), 0)
    rotated_key_slots = draw_rotated_key_slots(jax.random.fold_in(arg_keys[8], 71), 0)
    kept_value_slots = scatter_about(arg_keys[5], (TOTAL_SLOTS, KEY_VALUE_HEADS * HEAD_SIZE), 1.0, 6.0, ((0, 64), (1, 4)))
    router = jnp.clip(0.2 + 0.8 * jax.random.uniform(arg_keys[6], (TOTAL_SLOTS,), jnp.float32) ** shard_levels(arg_keys[6], (TOTAL_SLOTS,), ((0, 64),), -0.2, 0.2), 0.2, 1.0)
    out_weight = scatter_about(arg_keys[7], (QUERY_HEADS * HEAD_SIZE, D), (QUERY_HEADS * HEAD_SIZE) ** -0.5, 0.125, ((0, 4),))
    return {"residual": residual, "cotangent": cotangent, "kept_slots": kept_slots, "query": query, "rotated_key_slots": rotated_key_slots, "kept_value_slots": kept_value_slots, "router": router, "out_weight": out_weight}


neg_fill = -1e+30

def reference(residual, cotangent, kept_slots, query, rotated_key_slots, kept_value_slots, router, out_weight):
    score_scale = 1.0 / math.sqrt(HEAD_SIZE)
    query_group_width = QUERY_HEADS // KEY_VALUE_HEADS
    live_mask = kept_slots >= 0
    counts = lax.optimization_barrier(jnp.sum(live_mask.reshape(N_SEQ, MOST).astype(jnp.int32), axis=1))
    offsets = (jnp.cumsum(counts) - counts).astype(jnp.int32)
    slot_ids = jnp.arange(TOTAL_SLOTS, dtype=jnp.int32)
    kept_index = offsets[slot_ids // MOST] + slot_ids % MOST
    sort_key = jnp.where(live_mask, kept_index, KEPT_TOKENS + slot_ids)
    kept_token_sequence = jnp.argsort(sort_key)[:KEPT_TOKENS].astype(jnp.int32)
    token_rows = kept_token_sequence // MOST * TOK_DEV + kept_slots[kept_token_sequence]
    queries = query[kept_token_sequence].astype(jnp.float32).reshape(KEPT_TOKENS, QUERY_HEADS, HEAD_SIZE)
    key_tensor = jnp.repeat(rotated_key_slots[kept_token_sequence].astype(jnp.float32).reshape(KEPT_TOKENS, KEY_VALUE_HEADS, HEAD_SIZE), query_group_width, axis=1)
    value_tensor = jnp.repeat(kept_value_slots[kept_token_sequence].astype(jnp.float32).reshape(KEPT_TOKENS, KEY_VALUE_HEADS, HEAD_SIZE), query_group_width, axis=1)
    weight = router[kept_token_sequence]
    cot_rows = cotangent[token_rows]
    proj_grad = (weight[:, None] * cot_rows.astype(jnp.float32)).astype(jnp.bfloat16)
    attn_grad = jnp.dot(proj_grad, out_weight.T, preferred_element_type=jnp.float32).astype(jnp.bfloat16)
    attn_grad3 = attn_grad.astype(jnp.float32).reshape(KEPT_TOKENS, QUERY_HEADS, HEAD_SIZE)
    block_rows = math.gcd(KEPT_TOKENS, 256)
    key_pos = jnp.arange(KEPT_TOKENS, dtype=jnp.int32)

    def block_step(totals, block_start):
        key_total, value_total = totals
        query_block = lax.dynamic_slice_in_dim(queries, block_start, block_rows, 0)
        grad_block = lax.dynamic_slice_in_dim(attn_grad3, block_start, block_rows, 0)
        query_pos = block_start + jnp.arange(block_rows, dtype=jnp.int32)
        causal_mask = key_pos[None, :] <= query_pos[:, None]
        scores = jnp.einsum('qhd,khd->hqk', query_block, key_tensor) * score_scale
        scores = jnp.where(causal_mask[None], scores, neg_fill)
        exp_scores = jnp.exp(scores - lax.optimization_barrier(jnp.max(scores, axis=2, keepdims=True)))
        probs = exp_scores / lax.optimization_barrier(jnp.sum(exp_scores, axis=2, keepdims=True))
        probs_low = lax.optimization_barrier(probs.astype(jnp.bfloat16)).astype(jnp.float32)
        attended_block = jnp.einsum('hqk,khd->qhd', probs_low, value_tensor).astype(jnp.bfloat16)
        delta_row = lax.optimization_barrier(jnp.sum(grad_block * attended_block.astype(jnp.float32), axis=2))
        prob_grad = jnp.einsum('qhd,khd->hqk', grad_block, value_tensor)
        score_grad = probs * (prob_grad - jnp.transpose(delta_row)[:, :, None])
        score_low = lax.optimization_barrier(score_grad.astype(jnp.bfloat16)).astype(jnp.float32)
        query_grad = jnp.einsum('hqk,khd->qhd', score_low, key_tensor) * score_scale
        key_gradient = jnp.einsum('hqk,qhd->khd', score_low, query_block) * score_scale
        value_gradient = jnp.einsum('hqk,qhd->khd', probs_low, grad_block)
        key_gradient = key_gradient.reshape(KEPT_TOKENS, KEY_VALUE_HEADS, query_group_width, HEAD_SIZE).sum(axis=2)
        value_gradient = value_gradient.reshape(KEPT_TOKENS, KEY_VALUE_HEADS, query_group_width, HEAD_SIZE).sum(axis=2)
        return ((key_total + key_gradient, value_total + value_gradient), (attended_block, query_grad.astype(jnp.bfloat16)))
    block_starts = jnp.arange(0, KEPT_TOKENS, block_rows, dtype=jnp.int32)
    empty_key_rows = jnp.zeros((KEPT_TOKENS, KEY_VALUE_HEADS, HEAD_SIZE), jnp.float32)
    (key_gradient_total, value_gradient_total), (attended_blocks, query_blocks) = lax.scan(block_step, (empty_key_rows, empty_key_rows), block_starts)
    attended = attended_blocks.reshape(KEPT_TOKENS, QUERY_HEADS * HEAD_SIZE)
    projected = jnp.dot(attended, out_weight, preferred_element_type=jnp.float32)
    contribution = (weight[:, None] * projected).astype(jnp.bfloat16)
    updated = residual.astype(jnp.float32).at[token_rows].add(contribution.astype(jnp.float32)).astype(jnp.bfloat16)
    router_rows = lax.optimization_barrier(jnp.sum(cot_rows.astype(jnp.float32) * projected, axis=1))
    grad_router = jnp.zeros((TOTAL_SLOTS,), jnp.float32).at[kept_token_sequence].set(router_rows)
    grad_weight = jnp.dot(attended.T, proj_grad, preferred_element_type=jnp.float32).astype(jnp.bfloat16)
    grad_query = jnp.zeros((TOTAL_SLOTS, QUERY_HEADS * HEAD_SIZE), jnp.bfloat16).at[kept_token_sequence].set(query_blocks.reshape(KEPT_TOKENS, QUERY_HEADS * HEAD_SIZE))
    key_gradient_slots = jnp.zeros((TOTAL_SLOTS, KEY_VALUE_HEADS * HEAD_SIZE), jnp.bfloat16).at[kept_token_sequence].set(key_gradient_total.reshape(KEPT_TOKENS, KEY_VALUE_HEADS * HEAD_SIZE).astype(jnp.bfloat16))
    value_gradient_slots = jnp.zeros((TOTAL_SLOTS, KEY_VALUE_HEADS * HEAD_SIZE), jnp.bfloat16).at[kept_token_sequence].set(value_gradient_total.reshape(KEPT_TOKENS, KEY_VALUE_HEADS * HEAD_SIZE).astype(jnp.bfloat16))
    return (updated, grad_query, key_gradient_slots, value_gradient_slots, grad_router, grad_weight)
```

```python
import functools
import math

import jax
import jax.numpy as jnp
from jax import lax
from jax.experimental import pallas as pl
from jax.experimental.pallas import tpu as pltpu
from jax.sharding import PartitionSpec as P

HEAD = 128
NZ, NY, NC, NX = 8, 4, 2, 4
SLOTS = 64
ROWS = NZ * SLOTS
HEADS = 4
NEG = -1e30
DEAD = 100.0
SCALE = 1.0 / math.sqrt(HEAD)
LOG2E = math.log2(math.e)
BF = jnp.bfloat16
F32 = jnp.float32


def seq_move(a, dz=0, dy=0, dc=0):
    pairs = []
    for z in range(NZ):
        for y in range(NY):
            for c in range(NC):
                to = ((z + dz) % NZ * NY + (y + dy) % NY) * NC + (c ^ dc)
                pairs.append(((z * NY + y) * NC + c, to))
    return lax.ppermute(a, "seq", pairs)


def tp_move(a, dx):
    return lax.ppermute(a, "tp", [(x, (x + dx) % NX) for x in range(NX)])


def gather_z(a):
    up = seq_move(a, dz=1)
    down = seq_move(a, dz=-1)
    near = jnp.concatenate([up, a, down], axis=0)
    low = seq_move(near, dz=3)
    high = seq_move(near[: 2 * a.shape[0]], dz=-3)
    return jnp.concatenate([high, low, near], axis=0)


def dot(a, b, da, db):
    return lax.dot_general(a, b, (((da,), (db,)), ((), ())), preferred_element_type=F32)


def head_rows(ref):
    return jnp.concatenate([ref[:, h * HEAD : (h + 1) * HEAD] for h in range(HEADS)], axis=0)


def masked_scores(place, dy, dc, kv_ref, q_rows, diff):
    z, y, c = place[0], place[1], place[2]
    keys = kv_ref[:, :HEAD]
    scores = dot(keys, q_rows, 1, 1)
    own = (z * NY + y) * NC + c
    other_y = (y + NY - dy) & (NY - 1)
    other_c = c ^ dc
    out = []
    for k in range(NZ):
        shard = (((z + 2 + k) & (NZ - 1)) * NY + other_y) * NC + other_c
        live = kv_ref[k * SLOTS : (k + 1) * SLOTS, HEAD : HEAD + 1].astype(F32) < 0.5 * DEAD
        ok = jnp.logical_and(diff <= (own - shard) * SLOTS, live)
        piece = scores[k * SLOTS : (k + 1) * SLOTS] * (SCALE * LOG2E)
        out.append(jnp.where(ok, piece, NEG))
    return jnp.concatenate(out, axis=0)


def slot_difference():
    row = lax.broadcasted_iota(jnp.int32, (SLOTS, HEADS * SLOTS), 0)
    lane = lax.broadcasted_iota(jnp.int32, (SLOTS, HEADS * SLOTS), 1)
    return row - (lane & (SLOTS - 1))


BLOCKS = [(dy, dc) for dy in (0, 1, 3, 2) for dc in (0, 1)]


def forward_kernel(place, q_ref, *refs):
    kv_refs, (att_ref, lse_ref) = refs[:8], refs[8:]
    q_rows = head_rows(q_ref)
    diff = slot_difference()
    top = jnp.full((1, HEADS * SLOTS), NEG, F32)
    total = jnp.zeros((1, HEADS * SLOTS), F32)
    acc = jnp.zeros((HEAD, HEADS * SLOTS), F32)
    for (dy, dc), kv_ref in zip(BLOCKS, kv_refs):
        t = masked_scores(place, dy, dc, kv_ref, q_rows, diff)
        new_top = jnp.maximum(top, jnp.max(t, axis=0, keepdims=True))
        old = jnp.exp2(top - new_top)
        e = jnp.exp2(t - new_top)
        total = total * old + jnp.sum(e, axis=0, keepdims=True)
        acc = acc * old + dot(kv_ref[:, HEAD:], e.astype(BF), 0, 0)
        top = new_top
    out = (acc / total).T.astype(BF)
    for h in range(HEADS):
        att_ref[:, h * HEAD : (h + 1) * HEAD] = out[h * SLOTS : (h + 1) * SLOTS]
    lse_ref[...] = jnp.broadcast_to(top + jnp.log(total) * LOG2E, lse_ref.shape)


def backward_kernel(dy, first, last, place, q_ref, g_ref, att_ref, lse_ref, *refs):
    if first:
        kv_refs, outs = refs[:2], refs[2:]
    else:
        kv_refs, outs = refs[:2], refs[3:]
    q_rows = head_rows(q_ref)
    g_rows = head_rows(g_ref)
    att_rows = head_rows(att_ref)
    diff = slot_difference()
    delta = jnp.sum((g_rows.astype(F32) * att_rows.astype(F32)).T, axis=0, keepdims=True)
    lse = lse_ref[0:1]
    acc = jnp.zeros((HEAD, HEADS * SLOTS), F32) if first else refs[2][...]
    for dc in (1, 0):
        kv_ref, out_ref = kv_refs[dc], outs[dc]
        t = masked_scores(place, dy, dc, kv_ref, q_rows, diff)
        p = jnp.exp2(t - lse)
        dp = dot(kv_ref[:, HEAD:], g_rows, 1, 1)
        ds = (p * (dp - delta)).astype(BF)
        out_ref[:, :HEAD] = (dot(ds, q_rows, 1, 0) * SCALE).astype(BF)
        out_ref[:, HEAD:] = dot(p.astype(BF), g_rows, 1, 0).astype(BF)
        acc = acc + dot(kv_ref[:, :HEAD], ds, 0, 0)
    if last:
        grad = (acc * SCALE).T.astype(BF)
        for h in range(HEADS):
            outs[2][:, h * HEAD : (h + 1) * HEAD] = grad[h * SLOTS : (h + 1) * SLOTS]
    else:
        outs[2][...] = acc


def attn_grad_kernel(place, *refs):
    chunks, w_ref, g_ref, pieces, full = refs[:4], refs[4], refs[5], refs[6:14], refs[14]
    z, x = place[0], place[3]
    width = w_ref.shape[1] // NX
    acc = None
    for m in range(NX):
        start = pl.multiple_of(((x + NX - m) & (NX - 1)) * width, width)
        chunk = chunks[m][...]
        full[:, pl.ds(start, width)] = chunk
        term = dot(chunk, w_ref[:, pl.ds(start, width)], 1, 1)
        acc = term if acc is None else acc + term
    g_ref[...] = acc.astype(BF)
    part = w_ref.shape[1] // NZ
    for d in range(NZ):
        start = pl.multiple_of(((z + NZ - d) & (NZ - 1)) * part, part)
        pieces[d][...] = full[:, pl.ds(start, part)]


def project_kernel(place, att_ref, g_ref, w_ref, *outs):
    x = place[3]
    width = w_ref.shape[1] // NX
    att = att_ref[...]
    delta = jnp.sum(att.astype(F32) * g_ref[...].astype(F32), axis=1, keepdims=True)
    high = delta.astype(BF).astype(F32)
    mid = (delta - high).astype(BF).astype(F32)
    low = delta - high - mid
    lane = lax.broadcasted_iota(jnp.int32, (SLOTS, HEAD), 1)
    zero = jnp.zeros((), F32)
    extra = jnp.where(lane == 0, high, jnp.where(lane == 1, mid, jnp.where(lane == 2, low, zero)))
    for m in range(NX):
        start = pl.multiple_of(((x + NX - m) & (NX - 1)) * width, width)
        outs[m][:, :width] = dot(att, w_ref[:, pl.ds(start, width)], 1, 0).astype(BF)
        outs[m][:, width:] = extra.astype(BF)


def weight_kernel(place, att_ref, *refs):
    pieces, outs, rows = refs[:8], refs[8:12], refs[12]
    y = place[1]
    for k in range(NZ):
        rows[k * SLOTS : (k + 1) * SLOTS] = pieces[(k + 2) % NZ][...]
    att = att_ref[...]
    width = rows.shape[1] // NY
    for m in range(NY):
        start = pl.multiple_of(((y + NY - m) & (NY - 1)) * width, width)
        outs[m][...] = dot(att, rows[:, pl.ds(start, width)], 0, 0).astype(BF)


VM = pl.BlockSpec(memory_space=pltpu.VMEM)
SM = pl.BlockSpec(memory_space=pltpu.SMEM)


def call(kernel, place, args, shapes, flops, scratch=(), limit=32):
    size = sum(math.prod(a.shape) * a.dtype.itemsize for a in args)
    size += sum(math.prod(s.shape) * s.dtype.itemsize for s in shapes)
    return pl.pallas_call(
        kernel,
        out_shape=shapes,
        in_specs=[SM] + [VM] * len(args),
        out_specs=[VM] * len(shapes),
        scratch_shapes=list(scratch),
        compiler_params=pltpu.CompilerParams(vmem_limit_bytes=limit * 1024 * 1024),
        cost_estimate=pl.CostEstimate(flops=flops, bytes_accessed=size, transcendentals=0),
    )(place, *args)


def shape(dims, dtype):
    return jax.ShapeDtypeStruct(dims, dtype)


def add(*parts):
    total = parts[0].astype(F32)
    for p in parts[1:]:
        total = total + p.astype(F32)
    return total


def on_device(
    residual, cotangent, kept_slots, query, rotated_key_slots, kept_value_slots, router, out_weight
):
    s = lax.axis_index("seq")
    z, y, c = s // (NY * NC), s // NC % NY, s % NC
    place = jnp.stack([z, y, c, lax.axis_index("tp")]).astype(jnp.int32)
    live = kept_slots >= 0
    live_col = live[:, None]

    kv = jnp.concatenate(
        [rotated_key_slots, jnp.where(live_col, kept_value_slots, jnp.asarray(DEAD, BF))], axis=1
    )
    kv_z = gather_z(kv)
    kv_y = {0: kv_z, 1: seq_move(kv_z, dy=1), 3: seq_move(kv_z, dy=-1), 2: seq_move(kv_z, dy=2)}
    kv_blocks = {}
    for dy in (0, 1, 3, 2):
        kv_blocks[dy, 0] = kv_y[dy]
        kv_blocks[dy, 1] = seq_move(kv_y[dy], dc=1)

    tokens = residual.shape[0]
    hot = (kept_slots[:, None] == jnp.arange(tokens, dtype=jnp.int32)[None, :]).astype(BF)
    weight_col = jnp.where(live, router, 0.0)[:, None]
    cot_rows = dot(hot, cotangent, 1, 0)
    proj_grad = (weight_col * cot_rows).astype(BF)
    chunks = [proj_grad] + [tp_move(proj_grad, m) for m in range(1, NX)]
    width = out_weight.shape[1]
    feats = out_weight.shape[0]
    attn_grad, *pieces = call(
        attn_grad_kernel,
        place,
        [*chunks, out_weight],
        [shape((SLOTS, feats), BF)] + [shape((SLOTS, width // NZ), BF)] * NZ,
        2 * SLOTS * width * feats,
        [pltpu.VMEM((SLOTS, width), BF)],
    )
    pieces = [pieces[0]] + [seq_move(pieces[d], dz=-d) for d in range(1, NZ)]

    attended, lse = call(
        forward_kernel,
        place,
        [query] + [kv_blocks[b] for b in BLOCKS],
        [shape((SLOTS, feats), BF), shape((8, HEADS * SLOTS), F32)],
        4 * 8 * ROWS * HEADS * SLOTS * HEAD,
    )

    projected = call(
        project_kernel,
        place,
        [attended, attn_grad, out_weight],
        [shape((SLOTS, width // NX + HEAD), BF)] * NX,
        2 * SLOTS * width * feats,
    )
    att_z = gather_z(attended)

    grad_query = None
    acc = []
    sums = {}
    order = (2, 1, 3, 0)
    for i, dy in enumerate(order):
        last = i == len(order) - 1
        own, other, out = call(
            functools.partial(backward_kernel, dy, i == 0, last),
            place,
            [query, attn_grad, attended, lse, kv_blocks[dy, 0], kv_blocks[dy, 1], *acc],
            [shape((ROWS, 2 * HEAD), BF)] * 2
            + [shape((SLOTS, feats), BF) if last else shape((HEAD, HEADS * SLOTS), F32)],
            10 * 2 * ROWS * HEADS * SLOTS * HEAD,
        )
        if last:
            grad_query = out
        acc = [out]
        sums[dy] = add(own, seq_move(other, dc=1)).astype(BF)
    parts = [sums[0]] + [seq_move(sums[m], dy=-m) for m in (2, 1, 3)]
    far_up = add(*[p[: 3 * SLOTS] for p in parts]).astype(BF)
    far_down = add(*[p[3 * SLOTS : 5 * SLOTS] for p in parts]).astype(BF)
    from_low = seq_move(far_up, dz=3)
    from_high = seq_move(far_down, dz=-3)
    near = [p[5 * SLOTS :] for p in parts]
    below = add(*[p[:SLOTS] for p in near], from_low[:SLOTS]).astype(BF)
    above = add(
        *[p[2 * SLOTS :] for p in near], from_low[2 * SLOTS :], from_high[SLOTS:]
    ).astype(BF)
    here = add(
        *[p[SLOTS : 2 * SLOTS] for p in near],
        from_low[SLOTS : 2 * SLOTS],
        from_high[:SLOTS],
        seq_move(below, dz=-1),
        seq_move(above, dz=1),
    )
    here = jnp.where(live_col, here, 0.0).astype(BF)

    weight_parts = call(
        weight_kernel,
        place,
        [att_z, *pieces],
        [shape((feats, width // NZ // NY), BF)] * NY,
        2 * ROWS * feats * (width // NZ),
        [pltpu.VMEM((ROWS, width // NZ), BF)],
    )
    weight_sum = add(
        weight_parts[0], *[seq_move(weight_parts[m], dy=-m) for m in range(1, NY)]
    ).astype(BF)
    weight_sum = add(weight_sum, seq_move(weight_sum, dc=1))
    half = width // NZ // NY // NC
    grad_weight = lax.dynamic_slice_in_dim(weight_sum, c * half, half, 1).astype(BF)

    mine = add(projected[0], *[tp_move(projected[m], -m) for m in range(1, NX)])
    contribution = (weight_col * mine[:, : width // NX]).astype(BF)
    router_sum = mine[:, width // NX] + mine[:, width // NX + 1] + mine[:, width // NX + 2]
    grad_router = jnp.where(live, router_sum / router, 0.0)
    updated = (residual.astype(F32) + dot(hot, contribution, 0, 0)).astype(BF)
    grad_query = jnp.where(live_col, grad_query, jnp.zeros((), BF))
    return (updated, grad_query, here[:, :HEAD], here[:, HEAD:], grad_router, grad_weight)


def solution(mesh):
    return jax.shard_map(
        on_device,
        mesh=mesh,
        in_specs=(
            P("seq", "tp"),
            P("seq", "tp"),
            P("seq"),
            P("seq", "tp"),
            P("seq", "tp"),
            P("seq", "tp"),
            P("seq"),
            P("tp", None),
        ),
        out_specs=(
            P("seq", "tp"),
            P("seq", "tp"),
            P("seq", "tp"),
            P("seq", "tp"),
            P("seq"),
            P("tp", "seq"),
        ),
        check_vma=False,
    )
```

```python
import functools
import math

import jax
import jax.numpy as jnp
from jax import lax
from jax.experimental import pallas as pl
from jax.experimental.pallas import tpu as pltpu
from jax.sharding import PartitionSpec as P

HEAD = 128
NZ, NY, NC, NX = 8, 4, 2, 4
SLOTS = 64
ROWS = NZ * SLOTS
HEADS = 4
NEG = -1e30
DEAD = 100.0
SCALE = 1.0 / math.sqrt(HEAD)
LOG2E = math.log2(math.e)
BF = jnp.bfloat16
F32 = jnp.float32


def seq_move(a, dz=0, dy=0, dc=0):
    pairs = []
    for z in range(NZ):
        for y in range(NY):
            for c in range(NC):
                to = ((z + dz) % NZ * NY + (y + dy) % NY) * NC + (c ^ dc)
                pairs.append(((z * NY + y) * NC + c, to))
    return lax.ppermute(a, "seq", pairs)


def tp_move(a, dx):
    return lax.ppermute(a, "tp", [(x, (x + dx) % NX) for x in range(NX)])


def near_z(a):
    return jnp.concatenate([seq_move(a, dz=1), a, seq_move(a, dz=-1)], axis=0)


def far_z(near):
    low = seq_move(near, dz=3)
    high = seq_move(near[: 2 * near.shape[0] // 3], dz=-3)
    return high, low, near


def stage(values, *others):
    return lax.optimization_barrier((*values, *others))[: len(values)]


def dot(a, b, da, db):
    return lax.dot_general(a, b, (((da,), (db,)), ((), ())), preferred_element_type=F32)


def head_rows(ref):
    return jnp.concatenate([ref[:, h * HEAD : (h + 1) * HEAD] for h in range(HEADS)], axis=0)


def masked_scores(place, dy, dc, kv_ref, q_rows, diff):
    z, y, c = place[0], place[1], place[2]
    keys = kv_ref[:, :HEAD]
    scores = dot(keys, q_rows, 1, 1)
    own = (z * NY + y) * NC + c
    other_y = (y + NY - dy) & (NY - 1)
    other_c = c ^ dc
    out = []
    for k in range(NZ):
        shard = (((z + 2 + k) & (NZ - 1)) * NY + other_y) * NC + other_c
        live = kv_ref[k * SLOTS : (k + 1) * SLOTS, HEAD : HEAD + 1].astype(F32) < 0.5 * DEAD
        ok = jnp.logical_and(diff <= (own - shard) * SLOTS, live)
        piece = scores[k * SLOTS : (k + 1) * SLOTS] * (SCALE * LOG2E)
        out.append(jnp.where(ok, piece, NEG))
    return jnp.concatenate(out, axis=0)


def slot_difference():
    row = lax.broadcasted_iota(jnp.int32, (SLOTS, HEADS * SLOTS), 0)
    lane = lax.broadcasted_iota(jnp.int32, (SLOTS, HEADS * SLOTS), 1)
    return row - (lane & (SLOTS - 1))


FIRST = [(0, 0), (1, 0), (3, 0), (2, 0)]
SECOND = [(0, 1), (1, 1), (3, 1), (2, 1)]


def forward_kernel(blocks, first, last, place, q_ref, *refs):
    kv_refs, refs = refs[: len(blocks)], refs[len(blocks) :]
    q_rows = head_rows(q_ref)
    diff = slot_difference()
    if first:
        top = jnp.full((1, HEADS * SLOTS), NEG, F32)
        total = jnp.zeros((1, HEADS * SLOTS), F32)
        acc = jnp.zeros((HEAD, HEADS * SLOTS), F32)
    else:
        stats, acc = refs[0], refs[1][...]
        top, total = stats[0:1], stats[8:9]
        refs = refs[2:]
    for (dy, dc), kv_ref in zip(blocks, kv_refs):
        t = masked_scores(place, dy, dc, kv_ref, q_rows, diff)
        new_top = jnp.maximum(top, jnp.max(t, axis=0, keepdims=True))
        old = jnp.exp2(top - new_top)
        e = jnp.exp2(t - new_top)
        total = total * old + jnp.sum(e, axis=0, keepdims=True)
        acc = acc * old + dot(kv_ref[:, HEAD:], e.astype(BF), 0, 0)
        top = new_top
    if not last:
        refs[0][0:8] = jnp.broadcast_to(top, (8, HEADS * SLOTS))
        refs[0][8:16] = jnp.broadcast_to(total, (8, HEADS * SLOTS))
        refs[1][...] = acc
        return
    att_ref, lse_ref = refs
    out = (acc / total).T.astype(BF)
    for h in range(HEADS):
        att_ref[:, h * HEAD : (h + 1) * HEAD] = out[h * SLOTS : (h + 1) * SLOTS]
    lse_ref[...] = jnp.broadcast_to(top + jnp.log(total) * LOG2E, lse_ref.shape)


STEPS = (0, 1, 3, 2)


def backward_kernel(dc, place, q_ref, g_ref, att_ref, lse_ref, *refs):
    kv_refs, refs = refs[:NY], refs[NY:]
    q_rows = head_rows(q_ref)
    g_rows = head_rows(g_ref)
    att_rows = head_rows(att_ref)
    diff = slot_difference()
    delta = jnp.sum((g_rows.astype(F32) * att_rows.astype(F32)).T, axis=0, keepdims=True)
    lse = lse_ref[0:1]
    if dc == 1:
        acc = jnp.zeros((HEAD, HEADS * SLOTS), F32)
        outs = [refs[0].at[i * ROWS : (i + 1) * ROWS] for i in range(NY)]
    else:
        acc, refs = refs[0][...], refs[1:]
        outs = refs[:NY]
    for dy, kv_ref, out_ref in zip(STEPS, kv_refs, outs):
        t = masked_scores(place, dy, dc, kv_ref, q_rows, diff)
        p = jnp.exp2(t - lse)
        dp = dot(kv_ref[:, HEAD:], g_rows, 1, 1)
        ds = (p * (dp - delta)).astype(BF)
        out_ref[:, :HEAD] = (dot(ds, q_rows, 1, 0) * SCALE).astype(BF)
        out_ref[:, HEAD:] = dot(p.astype(BF), g_rows, 1, 0).astype(BF)
        acc = acc + dot(kv_ref[:, :HEAD], ds, 0, 0)
    if dc == 1:
        refs[1][...] = acc
    else:
        grad = (acc * SCALE).T.astype(BF)
        for h in range(HEADS):
            refs[NY][:, h * HEAD : (h + 1) * HEAD] = grad[h * SLOTS : (h + 1) * SLOTS]


def attn_grad_kernel(place, *refs):
    chunks, w_ref, g_ref, groups, full = refs[:4], refs[4], refs[5], refs[6:9], refs[9]
    z, x = place[0], place[3]
    width = w_ref.shape[1] // NX
    acc = None
    for m in range(NX):
        start = pl.multiple_of(((x + NX - m) & (NX - 1)) * width, width)
        chunk = chunks[m][...]
        full[:, pl.ds(start, width)] = chunk
        term = dot(chunk, w_ref[:, pl.ds(start, width)], 1, 1)
        acc = term if acc is None else acc + term
    g_ref[...] = acc.astype(BF)
    part = w_ref.shape[1] // NZ
    for group, offsets in zip(groups, ((2, 3, 4), (5, 6), (7, 8, 9))):
        for i, d in enumerate(offsets):
            start = pl.multiple_of(((z + d) & (NZ - 1)) * part, part)
            group[i * SLOTS : (i + 1) * SLOTS] = full[:, pl.ds(start, part)]


def project_kernel(place, att_ref, g_ref, w_ref, *outs):
    x = place[3]
    width = w_ref.shape[1] // NX
    att = att_ref[...]
    delta = jnp.sum(att.astype(F32) * g_ref[...].astype(F32), axis=1, keepdims=True)
    high = delta.astype(BF).astype(F32)
    mid = (delta - high).astype(BF).astype(F32)
    low = delta - high - mid
    lane = lax.broadcasted_iota(jnp.int32, (SLOTS, HEAD), 1)
    zero = jnp.zeros((), F32)
    extra = jnp.where(lane == 0, high, jnp.where(lane == 1, mid, jnp.where(lane == 2, low, zero)))
    for m in range(NX):
        start = pl.multiple_of(((x + NX - m) & (NX - 1)) * width, width)
        outs[m][:, :width] = dot(att, w_ref[:, pl.ds(start, width)], 1, 0).astype(BF)
        outs[m][:, width:] = extra.astype(BF)


def weight_kernel(place, high, low, near, own, from_low, from_high, from_below, from_above, *refs):
    outs, att, rows = refs[:NY], refs[NY], refs[NY + 1]
    y = place[1]
    att[: 2 * SLOTS] = high[...]
    att[2 * SLOTS : 5 * SLOTS] = low[...]
    att[5 * SLOTS :] = near[...]
    order = (
        (from_below, 2),
        (from_high, 0),
        (from_below, 1),
        (from_low, 1),
        (from_above, 1),
        (from_below, 0),
        (own, 1),
        (from_above, 0),
    )
    for k, (ref, i) in enumerate(order):
        rows[k * SLOTS : (k + 1) * SLOTS] = ref[i * SLOTS : (i + 1) * SLOTS]
    width = rows.shape[1] // NY
    for m in range(NY):
        start = pl.multiple_of(((y + NY - m) & (NY - 1)) * width, width)
        outs[m][...] = dot(att[...], rows[:, pl.ds(start, width)], 0, 0).astype(BF)


VM = pl.BlockSpec(memory_space=pltpu.VMEM)
SM = pl.BlockSpec(memory_space=pltpu.SMEM)


def call(kernel, place, args, shapes, flops, scratch=(), limit=32):
    size = sum(math.prod(a.shape) * a.dtype.itemsize for a in args)
    size += sum(math.prod(s.shape) * s.dtype.itemsize for s in shapes)
    return pl.pallas_call(
        kernel,
        out_shape=shapes,
        in_specs=[SM] + [VM] * len(args),
        out_specs=[VM] * len(shapes),
        scratch_shapes=list(scratch),
        compiler_params=pltpu.CompilerParams(vmem_limit_bytes=limit * 1024 * 1024),
        cost_estimate=pl.CostEstimate(flops=flops, bytes_accessed=size, transcendentals=0),
    )(place, *args)


def shape(dims, dtype):
    return jax.ShapeDtypeStruct(dims, dtype)


def add(*parts):
    total = parts[0].astype(F32)
    for p in parts[1:]:
        total = total + p.astype(F32)
    return total


def on_device(
    residual, cotangent, kept_slots, query, rotated_key_slots, kept_value_slots, router, out_weight
):
    s = lax.axis_index("seq")
    z, y, c = s // (NY * NC), s // NC % NY, s % NC
    place = jnp.stack([z, y, c, lax.axis_index("tp")]).astype(jnp.int32)
    live = kept_slots >= 0
    live_col = live[:, None]

    tokens = residual.shape[0]
    width = out_weight.shape[1]
    feats = out_weight.shape[0]
    lanes = HEADS * SLOTS
    hot = (kept_slots[:, None] == jnp.arange(tokens, dtype=jnp.int32)[None, :]).astype(BF)
    weight_col = jnp.where(live, router, 0.0)[:, None]
    proj_grad = (weight_col * dot(hot, cotangent, 1, 0)).astype(BF)
    kv = jnp.concatenate(
        [rotated_key_slots, jnp.where(live_col, kept_value_slots, jnp.asarray(DEAD, BF))], axis=1
    )

    kv, proj_grad = stage((kv, proj_grad))
    kv_near = near_z(kv)
    chunks = {m: tp_move(proj_grad, m) for m in (1, 3, 2)}
    kv_near, chunks[1], chunks[3] = stage((kv_near, chunks[1], chunks[3]))
    kv_z = jnp.concatenate(far_z(kv_near), axis=0)
    attn_grad, far_up, far_down, own_part = call(
        attn_grad_kernel,
        place,
        [proj_grad, chunks[1], chunks[2], chunks[3], out_weight],
        [shape((SLOTS, feats), BF)]
        + [shape((n * SLOTS, width // NZ), BF) for n in (3, 2, 3)],
        2 * SLOTS * width * feats,
        [pltpu.VMEM((SLOTS, width), BF)],
    )
    kv_z, far_up, far_down = stage((kv_z, far_up, far_down))
    kv_y = [kv_z, seq_move(kv_z, dy=1), seq_move(kv_z, dy=-1), seq_move(kv_z, dy=2)]
    from_low = seq_move(far_up, dz=3)
    from_high = seq_move(far_down, dz=-3)
    kv_y = stage(kv_y, from_low, from_high)
    kv_c = [seq_move(a, dc=1) for a in kv_y]
    state = call(
        functools.partial(forward_kernel, FIRST, True, False),
        place,
        [query, *kv_y],
        [shape((16, lanes), F32), shape((HEAD, lanes), F32)],
        4 * len(FIRST) * ROWS * lanes * HEAD,
    )
    attended, lse = call(
        functools.partial(forward_kernel, SECOND, False, True),
        place,
        [query, *stage(kv_c, *state), *state],
        [shape((SLOTS, feats), BF), shape((8, lanes), F32)],
        4 * len(SECOND) * ROWS * lanes * HEAD,
    )
    n = SLOTS
    for_above = jnp.concatenate([own_part[2 * n :], from_low[2 * n :], from_high[n:]], axis=0)
    for_below = jnp.concatenate([own_part[:n], from_low[:n]], axis=0)
    for_above, for_below = stage((for_above, for_below), attended)
    att_near = near_z(attended)
    from_below = seq_move(for_above, dz=1)
    from_above = seq_move(for_below, dz=-1)
    other, acc = call(
        functools.partial(backward_kernel, 1),
        place,
        [query, attn_grad, attended, lse, *kv_c],
        [shape((NY * ROWS, 2 * HEAD), BF), shape((HEAD, lanes), F32)],
        10 * NY * ROWS * lanes * HEAD,
    )
    other, acc = stage((other, acc))
    theirs = seq_move(other, dc=1)
    *own, grad_query = call(
        functools.partial(backward_kernel, 0),
        place,
        [query, attn_grad, attended, lse, *kv_y, acc],
        [shape((ROWS, 2 * HEAD), BF)] * NY + [shape((SLOTS, feats), BF)],
        10 * NY * ROWS * lanes * HEAD,
    )
    projected = call(
        project_kernel,
        place,
        [attended, attn_grad, out_weight],
        [shape((SLOTS, width // NX + HEAD), BF)] * NX,
        2 * SLOTS * width * feats,
    )
    sums = [add(a, theirs[i * ROWS : (i + 1) * ROWS]).astype(BF) for i, a in enumerate(own)]
    *sums, att_near = stage((*sums, att_near), from_below, from_above, *projected)
    parts = [sums[0]] + [seq_move(sums[i], dy=-STEPS[i]) for i in range(1, NY)]
    att_z = far_z(att_near)
    projected = [projected[0]] + [tp_move(projected[m], -m) for m in (1, 3, 2)]
    weight_parts = call(
        weight_kernel,
        place,
        [*att_z, own_part, from_low, from_high, from_below, from_above],
        [shape((feats, width // NZ // NY), BF)] * NY,
        2 * ROWS * feats * (width // NZ),
        [pltpu.VMEM((ROWS, feats), BF), pltpu.VMEM((ROWS, width // NZ), BF)],
    )
    *parts, w0, w1, w2, w3 = stage((*parts, *weight_parts), *projected)
    sum_up = add(*[p[: 3 * n] for p in parts]).astype(BF)
    sum_down = add(*[p[3 * n : 5 * n] for p in parts]).astype(BF)
    sum_low = seq_move(sum_up, dz=3)
    sum_high = seq_move(sum_down, dz=-3)
    weight_sum = add(
        w0, seq_move(w1, dy=-1), seq_move(w2, dy=-2), seq_move(w3, dy=-3)
    ).astype(BF)
    near = [p[5 * n :] for p in parts]
    below = add(*[p[:n] for p in near], sum_low[:n]).astype(BF)
    above = add(*[p[2 * n :] for p in near], sum_low[2 * n :], sum_high[n:]).astype(BF)
    here = add(*[p[n : 2 * n] for p in near], sum_low[n : 2 * n], sum_high[:n])
    below, above, here, weight_sum = stage((below, above, here, weight_sum))
    weight_sum = add(weight_sum, seq_move(weight_sum, dc=1))
    here = add(here, seq_move(below, dz=-1), seq_move(above, dz=1))
    here = jnp.where(live_col, here, 0.0).astype(BF)
    half = width // NZ // NY // NC
    grad_weight = lax.dynamic_slice_in_dim(weight_sum, c * half, half, 1).astype(BF)

    mine = add(*projected)
    contribution = (weight_col * mine[:, : width // NX]).astype(BF)
    router_sum = mine[:, width // NX] + mine[:, width // NX + 1] + mine[:, width // NX + 2]
    grad_router = jnp.where(live, router_sum / router, 0.0)
    updated = (residual.astype(F32) + dot(hot, contribution, 0, 0)).astype(BF)
    grad_query = jnp.where(live_col, grad_query, jnp.zeros((), BF))
    return (updated, grad_query, here[:, :HEAD], here[:, HEAD:], grad_router, grad_weight)


def solution(mesh):
    return jax.shard_map(
        on_device,
        mesh=mesh,
        in_specs=(
            P("seq", "tp"),
            P("seq", "tp"),
            P("seq"),
            P("seq", "tp"),
            P("seq", "tp"),
            P("seq", "tp"),
            P("seq"),
            P("tp", None),
        ),
        out_specs=(
            P("seq", "tp"),
            P("seq", "tp"),
            P("seq", "tp"),
            P("seq", "tp"),
            P("seq"),
            P("tp", "seq"),
        ),
        check_vma=False,
    )
```

```python
import functools
import math

import jax
import jax.numpy as jnp
from jax import lax
from jax.experimental import pallas as pl
from jax.experimental.pallas import tpu as pltpu
from jax.sharding import PartitionSpec as P

HEAD = 128
NZ, NY, NC, NX = 8, 4, 2, 4
SLOTS = 64
ROWS = NZ * SLOTS
HEADS = 4
NEG = -1e30
DEAD = 100.0
SCALE = 1.0 / math.sqrt(HEAD)
LOG2E = math.log2(math.e)
BF = jnp.bfloat16
F32 = jnp.float32


def seq_move(a, dz=0, dy=0, dc=0):
    pairs = []
    for z in range(NZ):
        for y in range(NY):
            for c in range(NC):
                to = ((z + dz) % NZ * NY + (y + dy) % NY) * NC + (c ^ dc)
                pairs.append(((z * NY + y) * NC + c, to))
    return lax.ppermute(a, "seq", pairs)


def tp_move(a, dx):
    return lax.ppermute(a, "tp", [(x, (x + dx) % NX) for x in range(NX)])


LINES = [[(k * NY + j) * NC + i for k in range(NZ)] for j in range(NY) for i in range(NC)]


def exchange_z(a):
    return lax.all_to_all(
        a, "seq", split_axis=0, concat_axis=0, axis_index_groups=LINES, tiled=True
    )


def sum_far(parts):
    n = SLOTS
    up = add(*[p[: 3 * n] for p in parts]).astype(BF)
    down = add(*[p[3 * n : 5 * n] for p in parts]).astype(BF)
    return seq_move(up, dz=3), seq_move(down, dz=-3), [p[5 * n :] for p in parts]


def sum_near(low, high, near):
    n = SLOTS
    below = add(*[p[:n] for p in near], low[:n]).astype(BF)
    above = add(*[p[2 * n :] for p in near], low[2 * n :], high[n:]).astype(BF)
    return below, above, add(*[p[n : 2 * n] for p in near], low[n : 2 * n], high[:n])


def sum_last(below, above, here):
    return add(here, seq_move(below, dz=-1), seq_move(above, dz=1))


def stage(values, *others):
    return lax.optimization_barrier((*values, *others))[: len(values)]


def dot(a, b, da, db):
    return lax.dot_general(a, b, (((da,), (db,)), ((), ())), preferred_element_type=F32)


def head_rows(ref):
    return jnp.concatenate([ref[:, h * HEAD : (h + 1) * HEAD] for h in range(HEADS)], axis=0)


def masked_scores(place, dy, dc, kv_ref, q_rows, diff):
    z, y, c = place[0], place[1], place[2]
    keys = kv_ref[:, :HEAD]
    scores = dot(keys, q_rows, 1, 1)
    own = (z * NY + y) * NC + c
    other_y = (y + NY - dy) & (NY - 1)
    other_c = c ^ dc
    out = []
    for k in range(NZ):
        shard = (k * NY + other_y) * NC + other_c
        live = kv_ref[k * SLOTS : (k + 1) * SLOTS, HEAD : HEAD + 1].astype(F32) < 0.5 * DEAD
        ok = jnp.logical_and(diff <= (own - shard) * SLOTS, live)
        piece = scores[k * SLOTS : (k + 1) * SLOTS] * (SCALE * LOG2E)
        out.append(jnp.where(ok, piece, NEG))
    return jnp.concatenate(out, axis=0)


def slot_difference():
    row = lax.broadcasted_iota(jnp.int32, (SLOTS, HEADS * SLOTS), 0)
    lane = lax.broadcasted_iota(jnp.int32, (SLOTS, HEADS * SLOTS), 1)
    return row - (lane & (SLOTS - 1))


FIRST = [(0, 0), (1, 0), (3, 0), (2, 0)]
SECOND = [(0, 1), (1, 1), (3, 1), (2, 1)]


def forward_kernel(blocks, first, last, place, q_ref, *refs):
    kv_refs, refs = refs[: len(blocks)], refs[len(blocks) :]
    q_rows = head_rows(q_ref)
    diff = slot_difference()
    if first:
        top = jnp.full((1, HEADS * SLOTS), NEG, F32)
        total = jnp.zeros((1, HEADS * SLOTS), F32)
        acc = jnp.zeros((HEAD, HEADS * SLOTS), F32)
    else:
        stats, acc = refs[0], refs[1][...]
        top, total = stats[0:1], stats[8:9]
        refs = refs[2:]
    for (dy, dc), kv_ref in zip(blocks, kv_refs):
        t = masked_scores(place, dy, dc, kv_ref, q_rows, diff)
        new_top = jnp.maximum(top, jnp.max(t, axis=0, keepdims=True))
        old = jnp.exp2(top - new_top)
        e = jnp.exp2(t - new_top)
        total = total * old + jnp.sum(e, axis=0, keepdims=True)
        acc = acc * old + dot(kv_ref[:, HEAD:], e.astype(BF), 0, 0)
        top = new_top
    if last:
        pieces, refs = refs[:NY], refs[NY:]
    if not last:
        refs[0][0:8] = jnp.broadcast_to(top, (8, HEADS * SLOTS))
        refs[0][8:16] = jnp.broadcast_to(total, (8, HEADS * SLOTS))
        refs[1][...] = acc
        return
    att_ref, lse_ref, rows = refs[0], refs[1], refs[2:]
    out = (acc / total).T.astype(BF)
    for h in range(HEADS):
        for ref in (att_ref, *rows):
            ref[:, h * HEAD : (h + 1) * HEAD] = out[h * SLOTS : (h + 1) * SLOTS]
    for ref, piece in zip(rows, pieces):
        ref[:, HEADS * HEAD :] = piece[...]
    lse_ref[...] = jnp.broadcast_to(top + jnp.log(total) * LOG2E, lse_ref.shape)


STEPS = (0, 1, 3, 2)


def backward_kernel(dc, place, q_ref, g_ref, att_ref, lse_ref, *refs):
    kv_refs, refs = refs[:NY], refs[NY:]
    q_rows = head_rows(q_ref)
    g_rows = head_rows(g_ref)
    att_rows = head_rows(att_ref)
    diff = slot_difference()
    delta = jnp.sum((g_rows.astype(F32) * att_rows.astype(F32)).T, axis=0, keepdims=True)
    lse = lse_ref[0:1]
    if dc == 1:
        acc = jnp.zeros((HEAD, HEADS * SLOTS), F32)
        outs = [refs[0].at[i * ROWS : (i + 1) * ROWS] for i in range(NY)]
    else:
        acc, refs = refs[0][...], refs[1:]
        outs = refs[:NY]
    for dy, kv_ref, out_ref in zip(STEPS, kv_refs, outs):
        t = masked_scores(place, dy, dc, kv_ref, q_rows, diff)
        p = jnp.exp2(t - lse)
        dp = dot(kv_ref[:, HEAD:], g_rows, 1, 1)
        ds = (p * (dp - delta)).astype(BF)
        key_grad = (dot(ds, q_rows, 1, 0) * SCALE).astype(BF)
        value_grad = dot(p.astype(BF), g_rows, 1, 0).astype(BF)
        for k in range(NZ):
            start = ((k + NZ - 2 - place[0]) & (NZ - 1)) * SLOTS
            at = pl.ds(pl.multiple_of(start, SLOTS), SLOTS)
            out_ref[at, :HEAD] = key_grad[k * SLOTS : (k + 1) * SLOTS]
            out_ref[at, HEAD:] = value_grad[k * SLOTS : (k + 1) * SLOTS]
        acc = acc + dot(kv_ref[:, :HEAD], ds, 0, 0)
    if dc == 1:
        refs[1][...] = acc
    else:
        grad = (acc * SCALE).T.astype(BF)
        for h in range(HEADS):
            refs[NY][:, h * HEAD : (h + 1) * HEAD] = grad[h * SLOTS : (h + 1) * SLOTS]


def attn_grad_kernel(place, *refs):
    chunks, w_ref, g_ref, pieces, full = refs[:4], refs[4], refs[5], refs[6:10], refs[10]
    z, y, c, x = place[0], place[1], place[2], place[3]
    width = w_ref.shape[1] // NX
    acc = None
    for m in range(NX):
        start = pl.multiple_of(((x + NX - m) & (NX - 1)) * width, width)
        chunk = chunks[m][...]
        full[:, pl.ds(start, width)] = chunk
        term = dot(chunk, w_ref[:, pl.ds(start, width)], 1, 1)
        acc = term if acc is None else acc + term
    g_ref[...] = acc.astype(BF)
    part = w_ref.shape[1] // NZ
    half = HEAD // NC
    for m, piece in enumerate(pieces):
        for k in range(0, NZ, 2):
            pair = []
            for d in (k, k + 1):
                start = d * part + ((y + m) & (NY - 1)) * HEAD
                pair.append(full[:, pl.ds(pl.multiple_of(start, HEAD), HEAD)].astype(F32))
            first = jnp.concatenate([pair[0][:, :half], pair[1][:, :half]], axis=1)
            second = jnp.concatenate([pair[0][:, half:], pair[1][:, half:]], axis=1)
            mine = jnp.where(c == 0, first, second).astype(BF)
            other = jnp.where(c == 0, second, first).astype(BF)
            piece[:, k * half : (k + 2) * half] = mine
            piece[:, (NZ + k) * half : (NZ + k + 2) * half] = other


def project_kernel(place, att_ref, g_ref, w_ref, *outs):
    x = place[3]
    width = w_ref.shape[1] // NX
    att = att_ref[...]
    delta = jnp.sum(att.astype(F32) * g_ref[...].astype(F32), axis=1, keepdims=True)
    high = delta.astype(BF).astype(F32)
    mid = (delta - high).astype(BF).astype(F32)
    low = delta - high - mid
    lane = lax.broadcasted_iota(jnp.int32, (SLOTS, HEAD), 1)
    zero = jnp.zeros((), F32)
    extra = jnp.where(lane == 0, high, jnp.where(lane == 1, mid, jnp.where(lane == 2, low, zero)))
    for m in range(NX):
        start = pl.multiple_of(((x + NX - m) & (NX - 1)) * width, width)
        outs[m][:, :width] = dot(att, w_ref[:, pl.ds(start, width)], 1, 0).astype(BF)
        outs[m][:, width:] = extra.astype(BF)


def weight_kernel(place, *refs):
    rows, (mine, other), (att, cols) = refs[:NY], refs[NY : NY + 2], refs[NY + 2 :]
    feats = att.shape[1]
    for i, ref in enumerate(rows):
        att[i * SLOTS : (i + 1) * SLOTS] = ref[:, :feats]
        cols[i * SLOTS : (i + 1) * SLOTS] = ref[:, feats:]
    half = cols.shape[1] // NC
    mine[...] = dot(cols[:, :half], att[...], 0, 0).astype(BF)
    other[...] = dot(cols[:, half:], att[...], 0, 0).astype(BF)


VM = pl.BlockSpec(memory_space=pltpu.VMEM)
SM = pl.BlockSpec(memory_space=pltpu.SMEM)


def call(kernel, place, args, shapes, flops, scratch=(), limit=32):
    size = sum(math.prod(a.shape) * a.dtype.itemsize for a in args)
    size += sum(math.prod(s.shape) * s.dtype.itemsize for s in shapes)
    return pl.pallas_call(
        kernel,
        out_shape=shapes,
        in_specs=[SM] + [VM] * len(args),
        out_specs=[VM] * len(shapes),
        scratch_shapes=list(scratch),
        compiler_params=pltpu.CompilerParams(vmem_limit_bytes=limit * 1024 * 1024),
        cost_estimate=pl.CostEstimate(flops=flops, bytes_accessed=size, transcendentals=0),
    )(place, *args)


def shape(dims, dtype):
    return jax.ShapeDtypeStruct(dims, dtype)


def add(*parts):
    total = parts[0].astype(F32)
    for p in parts[1:]:
        total = total + p.astype(F32)
    return total


def on_device(
    residual, cotangent, kept_slots, query, rotated_key_slots, kept_value_slots, router, out_weight
):
    s = lax.axis_index("seq")
    z, y, c = s // (NY * NC), s // NC % NY, s % NC
    place = jnp.stack([z, y, c, lax.axis_index("tp")]).astype(jnp.int32)
    live = kept_slots >= 0
    live_col = live[:, None]

    tokens = residual.shape[0]
    width = out_weight.shape[1]
    feats = out_weight.shape[0]
    lanes = HEADS * SLOTS
    hot = (kept_slots[:, None] == jnp.arange(tokens, dtype=jnp.int32)[None, :]).astype(BF)
    weight_col = jnp.where(live, router, 0.0)[:, None]
    proj_grad = (weight_col * dot(hot, cotangent, 1, 0)).astype(BF)
    kv = jnp.concatenate(
        [rotated_key_slots, jnp.where(live_col, kept_value_slots, jnp.asarray(DEAD, BF))], axis=1
    )

    kv_z = exchange_z(jnp.broadcast_to(kv[None], (NZ, *kv.shape)).reshape(ROWS, 2 * HEAD))
    chunks = {m: tp_move(proj_grad, m) for m in (1, 3, 2)}
    kv_z, chunks[1], chunks[2], chunks[3] = stage((kv_z, chunks[1], chunks[2], chunks[3]))
    attn_grad, *pieces = call(
        attn_grad_kernel,
        place,
        [proj_grad, chunks[1], chunks[2], chunks[3], out_weight],
        [shape((SLOTS, feats), BF)] + [shape((SLOTS, width // NY), BF)] * NY,
        2 * SLOTS * width * feats,
        [pltpu.VMEM((SLOTS, width), BF)],
    )
    kv_y = [kv_z, seq_move(kv_z, dy=1), seq_move(kv_z, dy=-1), seq_move(kv_z, dy=2)]
    *kv_y, attn_grad = stage((*kv_y, attn_grad))
    kv_c = [seq_move(a, dc=1) for a in kv_y]
    state = call(
        functools.partial(forward_kernel, FIRST, True, False),
        place,
        [query, *kv_y],
        [shape((16, lanes), F32), shape((HEAD, lanes), F32)],
        4 * len(FIRST) * ROWS * lanes * HEAD,
    )
    attended, lse, *rows = call(
        functools.partial(forward_kernel, SECOND, False, True),
        place,
        [query, *stage(kv_c, *state), *state, *pieces],
        [shape((SLOTS, feats), BF), shape((8, lanes), F32)]
        + [shape((SLOTS, feats + width // NY), BF)] * NY,
        4 * len(SECOND) * ROWS * lanes * HEAD,
    )
    rows = [rows[0]] + [seq_move(rows[m], dy=m) for m in (1, 3, 2)]
    other, acc = call(
        functools.partial(backward_kernel, 1),
        place,
        [query, attn_grad, attended, lse, *kv_c],
        [shape((NY * ROWS, 2 * HEAD), BF), shape((HEAD, lanes), F32)],
        10 * NY * ROWS * lanes * HEAD,
    )
    other, acc = stage((other, acc))
    theirs = seq_move(other, dc=1)
    *own, grad_query = call(
        functools.partial(backward_kernel, 0),
        place,
        [query, attn_grad, attended, lse, *kv_y, acc],
        [shape((ROWS, 2 * HEAD), BF)] * NY + [shape((SLOTS, feats), BF)],
        10 * NY * ROWS * lanes * HEAD,
    )
    sums = [add(a, theirs[i * ROWS : (i + 1) * ROWS]).astype(BF) for i, a in enumerate(own)]
    sums = stage(sums)
    weight_mine, weight_other = call(
        weight_kernel,
        place,
        rows,
        [shape((width // NZ, feats), BF)] * 2,
        4 * NY * SLOTS * feats * (width // NZ),
        [pltpu.VMEM((NY * SLOTS, feats), BF), pltpu.VMEM((NY * SLOTS, width // NY), BF)],
    )
    weight_theirs = seq_move(weight_other, dc=1)
    parts = [sums[0]] + [seq_move(sums[i], dy=-STEPS[i]) for i in range(1, NY)]
    weight_sum = add(weight_mine, weight_theirs).astype(BF)
    weight_sum = exchange_z(weight_sum)
    parts = stage(parts)
    projected = call(
        project_kernel,
        place,
        [stage((attended,), *parts)[0], attn_grad, out_weight],
        [shape((SLOTS, width // NX + HEAD), BF)] * NX,
        2 * SLOTS * width * feats,
    )
    projected = [projected[0]] + [tp_move(projected[m], -m) for m in (1, 3, 2)]
    below, above, here = sum_near(*sum_far(parts))
    below, above = stage((below, above), *projected)
    here = jnp.where(live_col, sum_last(below, above, here), 0.0).astype(BF)
    grad_weight = add(*[weight_sum[k * SLOTS : (k + 1) * SLOTS] for k in range(NZ)]).astype(BF).T

    mine = add(*projected)
    contribution = (weight_col * mine[:, : width // NX]).astype(BF)
    router_sum = mine[:, width // NX] + mine[:, width // NX + 1] + mine[:, width // NX + 2]
    grad_router = jnp.where(live, router_sum / router, 0.0)
    updated = (residual.astype(F32) + dot(hot, contribution, 0, 0)).astype(BF)
    grad_query = jnp.where(live_col, grad_query, jnp.zeros((), BF))
    return (updated, grad_query, here[:, :HEAD], here[:, HEAD:], grad_router, grad_weight)


def solution(mesh):
    return jax.shard_map(
        on_device,
        mesh=mesh,
        in_specs=(
            P("seq", "tp"),
            P("seq", "tp"),
            P("seq"),
            P("seq", "tp"),
            P("seq", "tp"),
            P("seq", "tp"),
            P("seq"),
            P("tp", None),
        ),
        out_specs=(
            P("seq", "tp"),
            P("seq", "tp"),
            P("seq", "tp"),
            P("seq", "tp"),
            P("seq"),
            P("tp", "seq"),
        ),
        check_vma=False,
    )
```

```python
import functools
import math

import jax
import jax.numpy as jnp
from jax import lax
from jax.experimental import pallas as pl
from jax.experimental.pallas import tpu as pltpu
from jax.sharding import PartitionSpec as P

HEAD = 128
NZ, NY, NC, NX = 8, 4, 2, 4
SLOTS = 64
ROWS = NZ * SLOTS
HEADS = 4
NEG = -1e30
DEAD = 100.0
SCALE = 1.0 / math.sqrt(HEAD)
LOG2E = math.log2(math.e)
BF = jnp.bfloat16
F32 = jnp.float32


def seq_move(a, dz=0, dy=0, dc=0):
    pairs = []
    for z in range(NZ):
        for y in range(NY):
            for c in range(NC):
                to = ((z + dz) % NZ * NY + (y + dy) % NY) * NC + (c ^ dc)
                pairs.append(((z * NY + y) * NC + c, to))
    return lax.ppermute(a, "seq", pairs)


def tp_move(a, dx):
    return lax.ppermute(a, "tp", [(x, (x + dx) % NX) for x in range(NX)])


LINES = [[(k * NY + j) * NC + i for k in range(NZ)] for j in range(NY) for i in range(NC)]


def exchange_z(a):
    return lax.all_to_all(
        a, "seq", split_axis=0, concat_axis=0, axis_index_groups=LINES, tiled=True
    )


def sum_far(parts):
    n = SLOTS
    up = add(*[p[: 3 * n] for p in parts]).astype(BF)
    down = add(*[p[3 * n : 5 * n] for p in parts]).astype(BF)
    return seq_move(up, dz=3), seq_move(down, dz=-3), [p[5 * n :] for p in parts]


def sum_near(low, high, near):
    n = SLOTS
    below = add(*[p[:n] for p in near], low[:n]).astype(BF)
    above = add(*[p[2 * n :] for p in near], low[2 * n :], high[n:]).astype(BF)
    return below, above, add(*[p[n : 2 * n] for p in near], low[n : 2 * n], high[:n])


def sum_last(below, above, here):
    return add(here, seq_move(below, dz=-1), seq_move(above, dz=1))


def stage(values, *others):
    return lax.optimization_barrier((*values, *others))[: len(values)]


def dot(a, b, da, db):
    return lax.dot_general(a, b, (((da,), (db,)), ((), ())), preferred_element_type=F32)


def head_rows(ref):
    return jnp.concatenate([ref[:, h * HEAD : (h + 1) * HEAD] for h in range(HEADS)], axis=0)


def masked_scores(place, dy, dc, kv_ref, q_rows, diff):
    z, y, c = place[0], place[1], place[2]
    keys = kv_ref[:, :HEAD]
    scores = dot(keys, q_rows, 1, 1)
    own = (z * NY + y) * NC + c
    other_y = (y + NY - dy) & (NY - 1)
    other_c = c ^ dc
    out = []
    for k in range(NZ):
        shard = (k * NY + other_y) * NC + other_c
        live = kv_ref[k * SLOTS : (k + 1) * SLOTS, HEAD : HEAD + 1].astype(F32) < 0.5 * DEAD
        ok = jnp.logical_and(diff <= (own - shard) * SLOTS, live)
        piece = scores[k * SLOTS : (k + 1) * SLOTS] * (SCALE * LOG2E)
        out.append(jnp.where(ok, piece, NEG))
    return jnp.concatenate(out, axis=0)


def slot_difference():
    row = lax.broadcasted_iota(jnp.int32, (SLOTS, HEADS * SLOTS), 0)
    lane = lax.broadcasted_iota(jnp.int32, (SLOTS, HEADS * SLOTS), 1)
    return row - (lane & (SLOTS - 1))


FIRST = [(0, 0), (1, 0), (3, 0), (2, 0)]
SECOND = [(0, 1), (1, 1), (3, 1), (2, 1)]


def forward_kernel(blocks, first, last, place, q_ref, *refs):
    kv_refs, refs = refs[: len(blocks)], refs[len(blocks) :]
    q_rows = head_rows(q_ref)
    diff = slot_difference()
    if first:
        top = jnp.full((1, HEADS * SLOTS), NEG, F32)
        total = jnp.zeros((1, HEADS * SLOTS), F32)
        acc = jnp.zeros((HEAD, HEADS * SLOTS), F32)
    else:
        stats, acc = refs[0], refs[1][...]
        top, total = stats[0:1], stats[8:9]
        refs = refs[2:]
    ts = [
        masked_scores(place, dy, dc, kv_ref, q_rows, diff)
        for (dy, dc), kv_ref in zip(blocks, kv_refs)
    ]
    old_top = top
    for t in ts:
        top = jnp.maximum(top, jnp.max(t, axis=0, keepdims=True))
    old = jnp.exp2(old_top - top)
    total, acc = total * old, acc * old
    for t, kv_ref in zip(ts, kv_refs):
        e = jnp.exp2(t - top)
        total = total + jnp.sum(e, axis=0, keepdims=True)
        acc = acc + dot(kv_ref[:, HEAD:], e.astype(BF), 0, 0)
    if last:
        pieces, refs = refs[:NY], refs[NY:]
    if not last:
        refs[0][0:8] = jnp.broadcast_to(top, (8, HEADS * SLOTS))
        refs[0][8:16] = jnp.broadcast_to(total, (8, HEADS * SLOTS))
        refs[1][...] = acc
        return
    att_ref, lse_ref, rows = refs[0], refs[1], refs[2:]
    out = (acc / total).T.astype(BF)
    for h in range(HEADS):
        for ref in (att_ref, *rows):
            ref[:, h * HEAD : (h + 1) * HEAD] = out[h * SLOTS : (h + 1) * SLOTS]
    for ref, piece in zip(rows, pieces):
        ref[:, HEADS * HEAD :] = piece[...]
    lse_ref[...] = jnp.broadcast_to(top + jnp.log(total) * LOG2E, lse_ref.shape)


STEPS = (0, 1, 3, 2)


def backward_kernel(dc, place, q_ref, g_ref, att_ref, lse_ref, *refs):
    kv_refs, refs = refs[:NY], refs[NY:]
    q_rows = head_rows(q_ref)
    g_rows = head_rows(g_ref)
    att_rows = head_rows(att_ref)
    diff = slot_difference()
    delta = jnp.sum((g_rows.astype(F32) * att_rows.astype(F32)).T, axis=0, keepdims=True)
    lse = lse_ref[0:1]
    if dc == 1:
        acc = jnp.zeros((HEAD, HEADS * SLOTS), F32)
        outs = [refs[0].at[i * ROWS : (i + 1) * ROWS] for i in range(NY)]
    else:
        acc, refs = refs[0][...], refs[1:]
        outs = refs[:NY]
    for dy, kv_ref, out_ref in zip(STEPS, kv_refs, outs):
        t = masked_scores(place, dy, dc, kv_ref, q_rows, diff)
        p = jnp.exp2(t - lse)
        dp = dot(kv_ref[:, HEAD:], g_rows, 1, 1)
        ds = (p * (dp - delta)).astype(BF)
        key_grad = (dot(ds, q_rows, 1, 0) * SCALE).astype(BF)
        value_grad = dot(p.astype(BF), g_rows, 1, 0).astype(BF)
        for k in range(NZ):
            start = ((k + NZ - 2 - place[0]) & (NZ - 1)) * SLOTS
            at = pl.ds(pl.multiple_of(start, SLOTS), SLOTS)
            out_ref[at, :HEAD] = key_grad[k * SLOTS : (k + 1) * SLOTS]
            out_ref[at, HEAD:] = value_grad[k * SLOTS : (k + 1) * SLOTS]
        acc = acc + dot(kv_ref[:, :HEAD], ds, 0, 0)
    if dc == 1:
        refs[1][...] = acc
    else:
        grad = (acc * SCALE).T.astype(BF)
        for h in range(HEADS):
            refs[NY][:, h * HEAD : (h + 1) * HEAD] = grad[h * SLOTS : (h + 1) * SLOTS]


def attn_grad_kernel(place, *refs):
    chunks, w_ref, g_ref, pieces, full = refs[:4], refs[4], refs[5], refs[6:10], refs[10]
    z, y, c, x = place[0], place[1], place[2], place[3]
    width = w_ref.shape[1] // NX
    acc = None
    for m in range(NX):
        start = pl.multiple_of(((x + NX - m) & (NX - 1)) * width, width)
        chunk = chunks[m][...]
        full[:, pl.ds(start, width)] = chunk
        term = dot(chunk, w_ref[:, pl.ds(start, width)], 1, 1)
        acc = term if acc is None else acc + term
    g_ref[...] = acc.astype(BF)
    part = w_ref.shape[1] // NZ
    half = HEAD // NC
    for m, piece in enumerate(pieces):
        for k in range(0, NZ, 2):
            pair = []
            for d in (k, k + 1):
                start = d * part + ((y + m) & (NY - 1)) * HEAD
                pair.append(full[:, pl.ds(pl.multiple_of(start, HEAD), HEAD)].astype(F32))
            first = jnp.concatenate([pair[0][:, :half], pair[1][:, :half]], axis=1)
            second = jnp.concatenate([pair[0][:, half:], pair[1][:, half:]], axis=1)
            mine = jnp.where(c == 0, first, second).astype(BF)
            other = jnp.where(c == 0, second, first).astype(BF)
            piece[:, k * half : (k + 2) * half] = mine
            piece[:, (NZ + k) * half : (NZ + k + 2) * half] = other


def project_kernel(place, att_ref, g_ref, w_ref, *outs):
    x = place[3]
    width = w_ref.shape[1] // NX
    att = att_ref[...]
    delta = jnp.sum(att.astype(F32) * g_ref[...].astype(F32), axis=1, keepdims=True)
    high = delta.astype(BF).astype(F32)
    mid = (delta - high).astype(BF).astype(F32)
    low = delta - high - mid
    lane = lax.broadcasted_iota(jnp.int32, (SLOTS, HEAD), 1)
    zero = jnp.zeros((), F32)
    extra = jnp.where(lane == 0, high, jnp.where(lane == 1, mid, jnp.where(lane == 2, low, zero)))
    for m in range(NX):
        start = pl.multiple_of(((x + NX - m) & (NX - 1)) * width, width)
        outs[m][:, :width] = dot(att, w_ref[:, pl.ds(start, width)], 1, 0).astype(BF)
        outs[m][:, width:] = extra.astype(BF)


def weight_kernel(place, *refs):
    rows, (mine, other), (att, cols) = refs[:NY], refs[NY : NY + 2], refs[NY + 2 :]
    feats = att.shape[1]
    for i, ref in enumerate(rows):
        att[i * SLOTS : (i + 1) * SLOTS] = ref[:, :feats]
        cols[i * SLOTS : (i + 1) * SLOTS] = ref[:, feats:]
    half = cols.shape[1] // NC
    mine[...] = dot(cols[:, :half], att[...], 0, 0).astype(BF)
    other[...] = dot(cols[:, half:], att[...], 0, 0).astype(BF)


VM = pl.BlockSpec(memory_space=pltpu.VMEM)
SM = pl.BlockSpec(memory_space=pltpu.SMEM)


def call(kernel, place, args, shapes, flops, scratch=(), limit=32):
    size = sum(math.prod(a.shape) * a.dtype.itemsize for a in args)
    size += sum(math.prod(s.shape) * s.dtype.itemsize for s in shapes)
    return pl.pallas_call(
        kernel,
        out_shape=shapes,
        in_specs=[SM] + [VM] * len(args),
        out_specs=[VM] * len(shapes),
        scratch_shapes=list(scratch),
        compiler_params=pltpu.CompilerParams(vmem_limit_bytes=limit * 1024 * 1024),
        cost_estimate=pl.CostEstimate(flops=flops, bytes_accessed=size, transcendentals=0),
    )(place, *args)


def shape(dims, dtype):
    return jax.ShapeDtypeStruct(dims, dtype)


def add(*parts):
    total = parts[0].astype(F32)
    for p in parts[1:]:
        total = total + p.astype(F32)
    return total


def on_device(
    residual, cotangent, kept_slots, query, rotated_key_slots, kept_value_slots, router, out_weight
):
    s = lax.axis_index("seq")
    z, y, c = s // (NY * NC), s // NC % NY, s % NC
    place = jnp.stack([z, y, c, lax.axis_index("tp")]).astype(jnp.int32)
    live = kept_slots >= 0
    live_col = live[:, None]

    tokens = residual.shape[0]
    width = out_weight.shape[1]
    feats = out_weight.shape[0]
    lanes = HEADS * SLOTS
    hot = (kept_slots[:, None] == jnp.arange(tokens, dtype=jnp.int32)[None, :]).astype(BF)
    weight_col = jnp.where(live, router, 0.0)[:, None]
    proj_grad = (weight_col * dot(hot, cotangent, 1, 0)).astype(BF)
    kv = jnp.concatenate(
        [rotated_key_slots, jnp.where(live_col, kept_value_slots, jnp.asarray(DEAD, BF))], axis=1
    )

    kv_z = exchange_z(jnp.broadcast_to(kv[None], (NZ, *kv.shape)).reshape(ROWS, 2 * HEAD))
    chunks = {m: tp_move(proj_grad, m) for m in (1, 3, 2)}
    kv_z, chunks[1] = stage((kv_z, chunks[1]))
    attn_grad, *pieces = call(
        attn_grad_kernel,
        place,
        [proj_grad, chunks[1], chunks[2], chunks[3], out_weight],
        [shape((SLOTS, feats), BF)] + [shape((SLOTS, width // NY), BF)] * NY,
        2 * SLOTS * width * feats,
        [pltpu.VMEM((SLOTS, width), BF)],
    )
    kv_y = [kv_z, seq_move(kv_z, dy=1), seq_move(kv_z, dy=-1), seq_move(kv_z, dy=2)]
    *kv_y, attn_grad = stage((*kv_y, attn_grad))
    kv_c = [seq_move(a, dc=1) for a in kv_y]
    state = call(
        functools.partial(forward_kernel, FIRST, True, False),
        place,
        [query, *kv_y],
        [shape((16, lanes), F32), shape((HEAD, lanes), F32)],
        4 * len(FIRST) * ROWS * lanes * HEAD,
    )
    attended, lse, *rows = call(
        functools.partial(forward_kernel, SECOND, False, True),
        place,
        [query, *stage(kv_c, *state), *state, *pieces],
        [shape((SLOTS, feats), BF), shape((8, lanes), F32)]
        + [shape((SLOTS, feats + width // NY), BF)] * NY,
        4 * len(SECOND) * ROWS * lanes * HEAD,
    )
    rows = [rows[0]] + [seq_move(rows[m], dy=m) for m in (1, 3, 2)]
    other, acc = call(
        functools.partial(backward_kernel, 1),
        place,
        [query, attn_grad, attended, lse, *kv_c],
        [shape((NY * ROWS, 2 * HEAD), BF), shape((HEAD, lanes), F32)],
        10 * NY * ROWS * lanes * HEAD,
    )
    other, acc = stage((other, acc))
    theirs = seq_move(other, dc=1)
    *own, grad_query = call(
        functools.partial(backward_kernel, 0),
        place,
        [query, attn_grad, attended, lse, *kv_y, acc],
        [shape((ROWS, 2 * HEAD), BF)] * NY + [shape((SLOTS, feats), BF)],
        10 * NY * ROWS * lanes * HEAD,
    )
    sums = [add(a, theirs[i * ROWS : (i + 1) * ROWS]).astype(BF) for i, a in enumerate(own)]
    weight_mine, weight_other = call(
        weight_kernel,
        place,
        rows,
        [shape((width // NZ, feats), BF)] * 2,
        4 * NY * SLOTS * feats * (width // NZ),
        [pltpu.VMEM((NY * SLOTS, feats), BF), pltpu.VMEM((NY * SLOTS, width // NY), BF)],
    )
    weight_theirs = seq_move(weight_other, dc=1)
    parts = [sums[0]] + [seq_move(sums[i], dy=-STEPS[i]) for i in range(1, NY)]
    weight_sum = add(weight_mine, weight_theirs).astype(BF)
    weight_sum = exchange_z(weight_sum)
    parts = stage(parts)
    below, above, here = sum_near(*sum_far(parts))
    below, above = stage((below, above))
    projected = call(
        project_kernel,
        place,
        [stage((attended,), below, above)[0], attn_grad, out_weight],
        [shape((SLOTS, width // NX + HEAD), BF)] * NX,
        40 * SLOTS * width * feats,
    )
    projected = [projected[0]] + [tp_move(projected[m], -m) for m in (1, 3, 2)]
    here = jnp.where(live_col, sum_last(below, above, here), 0.0).astype(BF)
    grad_weight = add(*[weight_sum[k * SLOTS : (k + 1) * SLOTS] for k in range(NZ)]).astype(BF).T

    mine = add(*projected)
    contribution = (weight_col * mine[:, : width // NX]).astype(BF)
    router_sum = mine[:, width // NX] + mine[:, width // NX + 1] + mine[:, width // NX + 2]
    grad_router = jnp.where(live, router_sum / router, 0.0)
    updated = (residual.astype(F32) + dot(hot, contribution, 0, 0)).astype(BF)
    return (updated, grad_query, here[:, :HEAD], here[:, HEAD:], grad_router, grad_weight)


def solution(mesh):
    return jax.shard_map(
        on_device,
        mesh=mesh,
        in_specs=(
            P("seq", "tp"),
            P("seq", "tp"),
            P("seq"),
            P("seq", "tp"),
            P("seq", "tp"),
            P("seq", "tp"),
            P("seq"),
            P("tp", None),
        ),
        out_specs=(
            P("seq", "tp"),
            P("seq", "tp"),
            P("seq", "tp"),
            P("seq", "tp"),
            P("seq"),
            P("tp", "seq"),
        ),
        check_vma=False,
    )
```

```python
import functools
import math

import jax
import jax.numpy as jnp
from jax import lax
from jax.experimental import pallas as pl
from jax.experimental.pallas import tpu as pltpu
from jax.sharding import PartitionSpec as P

HEAD = 128
NZ, NY, NC, NX = 8, 4, 2, 4
SLOTS = 64
ROWS = NZ * SLOTS
HEADS = 4
NEG = -1e30
DEAD = 100.0
SCALE = 1.0 / math.sqrt(HEAD)
LOG2E = math.log2(math.e)
BF = jnp.bfloat16
F32 = jnp.float32


def seq_move(a, dz=0, dy=0, dc=0):
    pairs = []
    for z in range(NZ):
        for y in range(NY):
            for c in range(NC):
                to = ((z + dz) % NZ * NY + (y + dy) % NY) * NC + (c ^ dc)
                pairs.append(((z * NY + y) * NC + c, to))
    return lax.ppermute(a, "seq", pairs)


def tp_move(a, dx):
    return lax.ppermute(a, "tp", [(x, (x + dx) % NX) for x in range(NX)])


LINES = [[(k * NY + j) * NC + i for k in range(NZ)] for j in range(NY) for i in range(NC)]


def exchange_z(a):
    return lax.all_to_all(
        a, "seq", split_axis=0, concat_axis=0, axis_index_groups=LINES, tiled=True
    )


def sum_far(parts):
    n = SLOTS
    up = add(*[p[: 3 * n] for p in parts]).astype(BF)
    down = add(*[p[3 * n : 5 * n] for p in parts]).astype(BF)
    return seq_move(up, dz=3), seq_move(down, dz=-3), [p[5 * n :] for p in parts]


def sum_near(low, high, near):
    n = SLOTS
    below = add(*[p[:n] for p in near], low[:n]).astype(BF)
    above = add(*[p[2 * n :] for p in near], low[2 * n :], high[n:]).astype(BF)
    return below, above, add(*[p[n : 2 * n] for p in near], low[n : 2 * n], high[:n])


def sum_last(below, above, here):
    return add(here, seq_move(below, dz=-1), seq_move(above, dz=1))


def stage(values, *others):
    return lax.optimization_barrier((*values, *others))[: len(values)]


def dot(a, b, da, db):
    return lax.dot_general(a, b, (((da,), (db,)), ((), ())), preferred_element_type=F32)


def head_rows(ref):
    return jnp.concatenate([ref[:, h * HEAD : (h + 1) * HEAD] for h in range(HEADS)], axis=0)


def masked_scores(place, dy, dc, kv_ref, q_rows, diff):
    z, y, c = place[0], place[1], place[2]
    keys = kv_ref[:, :HEAD]
    scores = dot(keys, q_rows, 1, 1)
    own = (z * NY + y) * NC + c
    other_y = (y + NY - dy) & (NY - 1)
    other_c = c ^ dc
    out = []
    for k in range(NZ):
        shard = (k * NY + other_y) * NC + other_c
        live = kv_ref[k * SLOTS : (k + 1) * SLOTS, HEAD : HEAD + 1].astype(F32) < 0.5 * DEAD
        ok = jnp.logical_and(diff <= (own - shard) * SLOTS, live)
        piece = scores[k * SLOTS : (k + 1) * SLOTS] * (SCALE * LOG2E)
        out.append(jnp.where(ok, piece, NEG))
    return jnp.concatenate(out, axis=0)


def slot_difference():
    row = lax.broadcasted_iota(jnp.int32, (SLOTS, HEADS * SLOTS), 0)
    lane = lax.broadcasted_iota(jnp.int32, (SLOTS, HEADS * SLOTS), 1)
    return row - (lane & (SLOTS - 1))


FIRST = [(0, 0), (1, 0), (3, 0), (2, 0)]
SECOND = [(0, 1), (1, 1), (3, 1), (2, 1)]


def forward_kernel(blocks, first, last, place, q_ref, *refs):
    kv_refs, refs = refs[: len(blocks)], refs[len(blocks) :]
    q_rows = head_rows(q_ref)
    diff = slot_difference()
    if first:
        top = jnp.full((1, HEADS * SLOTS), NEG, F32)
        total = jnp.zeros((1, HEADS * SLOTS), F32)
        acc = jnp.zeros((HEAD, HEADS * SLOTS), F32)
    else:
        stats, acc = refs[0], refs[1][...]
        top, total = stats[0:1], stats[8:9]
        refs = refs[2:]
    ts = [
        masked_scores(place, dy, dc, kv_ref, q_rows, diff)
        for (dy, dc), kv_ref in zip(blocks, kv_refs)
    ]
    old_top = top
    for t in ts:
        top = jnp.maximum(top, jnp.max(t, axis=0, keepdims=True))
    old = jnp.exp2(old_top - top)
    total, acc = total * old, acc * old
    for t, kv_ref in zip(ts, kv_refs):
        e = jnp.exp2(t - top)
        total = total + jnp.sum(e, axis=0, keepdims=True)
        acc = acc + dot(kv_ref[:, HEAD:], e.astype(BF), 0, 0)
    if last:
        pieces, refs = refs[:NY], refs[NY:]
    if not last:
        refs[0][0:8] = jnp.broadcast_to(top, (8, HEADS * SLOTS))
        refs[0][8:16] = jnp.broadcast_to(total, (8, HEADS * SLOTS))
        refs[1][...] = acc
        return
    att_ref, lse_ref, rows = refs[0], refs[1], refs[2:]
    out = (acc / total).T.astype(BF)
    for h in range(HEADS):
        for ref in (att_ref, *rows):
            ref[:, h * HEAD : (h + 1) * HEAD] = out[h * SLOTS : (h + 1) * SLOTS]
    for ref, piece in zip(rows, pieces):
        ref[:, HEADS * HEAD :] = piece[...]
    lse_ref[...] = jnp.broadcast_to(top + jnp.log(total) * LOG2E, lse_ref.shape)


STEPS = (0, 1, 3, 2)


def backward_kernel(dc, place, q_ref, g_ref, att_ref, lse_ref, *refs):
    kv_refs, refs = refs[:NY], refs[NY:]
    q_rows = head_rows(q_ref)
    g_rows = head_rows(g_ref)
    att_rows = head_rows(att_ref)
    diff = slot_difference()
    delta = jnp.sum((g_rows.astype(F32) * att_rows.astype(F32)).T, axis=0, keepdims=True)
    lse = lse_ref[0:1]
    if dc == 1:
        acc = jnp.zeros((HEAD, HEADS * SLOTS), F32)
        outs = [refs[0].at[i * ROWS : (i + 1) * ROWS] for i in range(NY)]
    else:
        acc, refs = refs[0][...], refs[1:]
        outs = refs[:NY]
    for dy, kv_ref, out_ref in zip(STEPS, kv_refs, outs):
        t = masked_scores(place, dy, dc, kv_ref, q_rows, diff)
        p = jnp.exp2(t - lse)
        dp = dot(kv_ref[:, HEAD:], g_rows, 1, 1)
        ds = (p * (dp - delta)).astype(BF)
        key_grad = (dot(ds, q_rows, 1, 0) * SCALE).astype(BF)
        value_grad = dot(p.astype(BF), g_rows, 1, 0).astype(BF)
        for k in range(NZ):
            start = ((k + NZ - 2 - place[0]) & (NZ - 1)) * SLOTS
            at = pl.ds(pl.multiple_of(start, SLOTS), SLOTS)
            out_ref[at, :HEAD] = key_grad[k * SLOTS : (k + 1) * SLOTS]
            out_ref[at, HEAD:] = value_grad[k * SLOTS : (k + 1) * SLOTS]
        acc = acc + dot(kv_ref[:, :HEAD], ds, 0, 0)
    if dc == 1:
        refs[1][...] = acc
    else:
        grad = (acc * SCALE).T.astype(BF)
        for h in range(HEADS):
            refs[NY][:, h * HEAD : (h + 1) * HEAD] = grad[h * SLOTS : (h + 1) * SLOTS]


def attn_grad_kernel(place, *refs):
    chunks, w_ref, g_ref, pieces, full = refs[:4], refs[4], refs[5], refs[6:10], refs[10]
    z, y, c, x = place[0], place[1], place[2], place[3]
    width = w_ref.shape[1] // NX
    acc = None
    for m in range(NX):
        start = pl.multiple_of(((x + NX - m) & (NX - 1)) * width, width)
        chunk = chunks[m][...]
        full[:, pl.ds(start, width)] = chunk
        term = dot(chunk, w_ref[:, pl.ds(start, width)], 1, 1)
        acc = term if acc is None else acc + term
    g_ref[...] = acc.astype(BF)
    part = w_ref.shape[1] // NZ
    half = HEAD // NC
    for m, piece in enumerate(pieces):
        for k in range(0, NZ, 2):
            pair = []
            for d in (k, k + 1):
                start = d * part + ((y + m) & (NY - 1)) * HEAD
                pair.append(full[:, pl.ds(pl.multiple_of(start, HEAD), HEAD)].astype(F32))
            first = jnp.concatenate([pair[0][:, :half], pair[1][:, :half]], axis=1)
            second = jnp.concatenate([pair[0][:, half:], pair[1][:, half:]], axis=1)
            mine = jnp.where(c == 0, first, second).astype(BF)
            other = jnp.where(c == 0, second, first).astype(BF)
            piece[:, k * half : (k + 2) * half] = mine
            piece[:, (NZ + k) * half : (NZ + k + 2) * half] = other


def project_kernel(place, att_ref, g_ref, w_ref, *refs):
    outs, (blocks, sems) = refs[:NX], refs[NX:]
    x = place[3]
    width = w_ref.shape[1] // NX
    copies = []
    for m in range(NX):
        start = pl.multiple_of(((x + NX - m) & (NX - 1)) * width, width)
        copies.append(
            pltpu.make_async_copy(w_ref.at[:, pl.ds(start, width)], blocks.at[m], sems.at[m])
        )
        copies[m].start()
    att = att_ref[...]
    delta = jnp.sum(att.astype(F32) * g_ref[...].astype(F32), axis=1, keepdims=True)
    high = delta.astype(BF).astype(F32)
    mid = (delta - high).astype(BF).astype(F32)
    low = delta - high - mid
    lane = lax.broadcasted_iota(jnp.int32, (SLOTS, HEAD), 1)
    zero = jnp.zeros((), F32)
    extra = jnp.where(lane == 0, high, jnp.where(lane == 1, mid, jnp.where(lane == 2, low, zero)))
    for m in range(NX):
        copies[m].wait()
        outs[m][:, :width] = dot(att, blocks[m], 1, 0).astype(BF)
        outs[m][:, width:] = extra.astype(BF)


def weight_kernel(place, *refs):
    rows, (mine, other), (att, cols) = refs[:NY], refs[NY : NY + 2], refs[NY + 2 :]
    feats = att.shape[1]
    for i, ref in enumerate(rows):
        att[i * SLOTS : (i + 1) * SLOTS] = ref[:, :feats]
        cols[i * SLOTS : (i + 1) * SLOTS] = ref[:, feats:]
    half = cols.shape[1] // NC
    mine[...] = dot(cols[:, :half], att[...], 0, 0).astype(BF)
    other[...] = dot(cols[:, half:], att[...], 0, 0).astype(BF)


VM = pl.BlockSpec(memory_space=pltpu.VMEM)
SM = pl.BlockSpec(memory_space=pltpu.SMEM)


def call(kernel, place, args, shapes, flops, scratch=(), limit=32, last=VM):
    size = sum(math.prod(a.shape) * a.dtype.itemsize for a in args)
    size += sum(math.prod(s.shape) * s.dtype.itemsize for s in shapes)
    return pl.pallas_call(
        kernel,
        out_shape=shapes,
        in_specs=[SM] + [VM] * (len(args) - 1) + [last],
        out_specs=[VM] * len(shapes),
        scratch_shapes=list(scratch),
        compiler_params=pltpu.CompilerParams(vmem_limit_bytes=limit * 1024 * 1024),
        cost_estimate=pl.CostEstimate(flops=flops, bytes_accessed=size, transcendentals=0),
    )(place, *args)


def shape(dims, dtype):
    return jax.ShapeDtypeStruct(dims, dtype)


def add(*parts):
    total = parts[0].astype(F32)
    for p in parts[1:]:
        total = total + p.astype(F32)
    return total


def on_device(
    residual, cotangent, kept_slots, query, rotated_key_slots, kept_value_slots, router, out_weight
):
    s = lax.axis_index("seq")
    z, y, c = s // (NY * NC), s // NC % NY, s % NC
    place = jnp.stack([z, y, c, lax.axis_index("tp")]).astype(jnp.int32)
    live = kept_slots >= 0
    live_col = live[:, None]

    tokens = residual.shape[0]
    width = out_weight.shape[1]
    feats = out_weight.shape[0]
    lanes = HEADS * SLOTS
    hot = (kept_slots[:, None] == jnp.arange(tokens, dtype=jnp.int32)[None, :]).astype(BF)
    weight_col = jnp.where(live, router, 0.0)[:, None]
    proj_grad = (weight_col * dot(hot, cotangent, 1, 0)).astype(BF)
    kv = jnp.concatenate(
        [rotated_key_slots, jnp.where(live_col, kept_value_slots, jnp.asarray(DEAD, BF))], axis=1
    )

    kv_z = exchange_z(jnp.broadcast_to(kv[None], (NZ, *kv.shape)).reshape(ROWS, 2 * HEAD))
    chunks = {m: tp_move(proj_grad, m) for m in (1, 3, 2)}
    kv_z, chunks[1] = stage((kv_z, chunks[1]))
    attn_grad, *pieces = call(
        attn_grad_kernel,
        place,
        [proj_grad, chunks[1], chunks[2], chunks[3], out_weight],
        [shape((SLOTS, feats), BF)] + [shape((SLOTS, width // NY), BF)] * NY,
        2 * SLOTS * width * feats,
        [pltpu.VMEM((SLOTS, width), BF)],
    )
    kv_y = [kv_z, seq_move(kv_z, dy=1), seq_move(kv_z, dy=-1), seq_move(kv_z, dy=2)]
    *kv_y, attn_grad = stage((*kv_y, attn_grad))
    kv_c = [seq_move(a, dc=1) for a in kv_y]
    state = call(
        functools.partial(forward_kernel, FIRST, True, False),
        place,
        [query, *kv_y],
        [shape((16, lanes), F32), shape((HEAD, lanes), F32)],
        4 * len(FIRST) * ROWS * lanes * HEAD,
    )
    attended, lse, *rows = call(
        functools.partial(forward_kernel, SECOND, False, True),
        place,
        [query, *stage(kv_c, *state), *state, *pieces],
        [shape((SLOTS, feats), BF), shape((8, lanes), F32)]
        + [shape((SLOTS, feats + width // NY), BF)] * NY,
        4 * len(SECOND) * ROWS * lanes * HEAD,
    )
    rows = [rows[0]] + [seq_move(rows[m], dy=m) for m in (1, 3, 2)]
    other, acc = call(
        functools.partial(backward_kernel, 1),
        place,
        [query, attn_grad, attended, lse, *kv_c],
        [shape((NY * ROWS, 2 * HEAD), BF), shape((HEAD, lanes), F32)],
        10 * NY * ROWS * lanes * HEAD,
    )
    other, acc = stage((other, acc))
    theirs = seq_move(other, dc=1)
    *own, grad_query = call(
        functools.partial(backward_kernel, 0),
        place,
        [query, attn_grad, attended, lse, *kv_y, acc],
        [shape((ROWS, 2 * HEAD), BF)] * NY + [shape((SLOTS, feats), BF)],
        10 * NY * ROWS * lanes * HEAD,
    )
    sums = [add(a, theirs[i * ROWS : (i + 1) * ROWS]).astype(BF) for i, a in enumerate(own)]
    weight_mine, weight_other = call(
        weight_kernel,
        place,
        rows,
        [shape((width // NZ, feats), BF)] * 2,
        4 * NY * SLOTS * feats * (width // NZ),
        [pltpu.VMEM((NY * SLOTS, feats), BF), pltpu.VMEM((NY * SLOTS, width // NY), BF)],
    )
    weight_theirs = seq_move(weight_other, dc=1)
    parts = [sums[0]] + [seq_move(sums[i], dy=-STEPS[i]) for i in range(1, NY)]
    weight_sum = add(weight_mine, weight_theirs).astype(BF)
    weight_sum = exchange_z(weight_sum)
    parts = stage(parts)
    below, above, here = sum_near(*sum_far(parts))
    below, above = stage((below, above))
    projected = call(
        project_kernel,
        place,
        [stage((attended,), below, above)[0], attn_grad, out_weight],
        [shape((SLOTS, width // NX + HEAD), BF)] * NX,
        40 * SLOTS * width * feats,
        [pltpu.VMEM((NX, feats, width // NX), BF), pltpu.SemaphoreType.DMA((NX,))],
        last=pl.BlockSpec(memory_space=pltpu.HBM),
    )
    projected = [projected[0]] + [tp_move(projected[m], -m) for m in (1, 3, 2)]
    here = jnp.where(live_col, sum_last(below, above, here), 0.0).astype(BF)
    grad_weight = add(*[weight_sum[k * SLOTS : (k + 1) * SLOTS] for k in range(NZ)]).astype(BF).T

    mine = add(*projected)
    contribution = (weight_col * mine[:, : width // NX]).astype(BF)
    router_sum = mine[:, width // NX] + mine[:, width // NX + 1] + mine[:, width // NX + 2]
    grad_router = jnp.where(live, router_sum / router, 0.0)
    updated = (residual.astype(F32) + dot(hot, contribution, 0, 0)).astype(BF)
    return (updated, grad_query, here[:, :HEAD], here[:, HEAD:], grad_router, grad_weight)


def solution(mesh):
    return jax.shard_map(
        on_device,
        mesh=mesh,
        in_specs=(
            P("seq", "tp"),
            P("seq", "tp"),
            P("seq"),
            P("seq", "tp"),
            P("seq", "tp"),
            P("seq", "tp"),
            P("seq"),
            P("tp", None),
        ),
        out_specs=(
            P("seq", "tp"),
            P("seq", "tp"),
            P("seq", "tp"),
            P("seq", "tp"),
            P("seq"),
            P("tp", "seq"),
        ),
        check_vma=False,
    )
```
